256 devices in a mesh: row: 8 (over y, x_hi), col: 32 (over x_lo, z, core).
Axes of the slice: x: 4 (x_hi: 2, x_lo: 2; x = x_hi * 2 + x_lo), y: 4, z: 8, core: 2. Of those that a mesh axis runs over, the one named last changes fastest.
Arguments:
- inputs: bfloat16 [1024, 12288], P('col', 'row'), may hold values from -6 to 6
- out_grad: bfloat16 [1024, 12288], P('col', 'row'), may hold values from -6 to 6
- pre_act: bfloat16 [1024, 24576], P('row', 'col'), may hold values from -6 to 6
- w_up: bfloat16 [12288, 24576], P('row', 'col'), may hold values from -0.0546875 to 0.0546875
- w_down: bfloat16 [24576, 12288], P('col', 'row'), may hold values from -0.0390625 to 0.0390625
Outputs:
- input_grad: bfloat16 [1024, 12288], P('col', 'row')
- up_grad: bfloat16 [12288, 24576], P('row', 'col')
- down_grad: bfloat16 [24576, 12288], P('col', 'row')
The draws below stay inside these ranges and needn't reach their ends.
All inputs are finite; a program needn't handle non-finite values.
Results may differ from the reference program's by a relative error of at most 0.0051.
Values may be sent and summed in bfloat16 or wider, within the bound.
A program may use at most 128 MiB of HBM per device.

```python
import jax
import jax.numpy as jnp
from jax import lax

D = 12288
FF = 24576
TOKENS = 1024


def shard_levels(key, extent, split, smallest, largest):
    gain, own = 1.0, jax.random.fold_in(key, 6)
    for dim, parts in split:
        heights = jnp.exp(jax.random.uniform(jax.random.fold_in(own, dim), (parts,), jnp.float32, smallest / len(split), largest / len(split)))
        gain = gain * jnp.repeat(heights, extent[dim] // parts).reshape([-1 if axis == dim else 1 for axis in range(len(extent))])
    return gain


def noise(own_key, shape, spread, reach, shards=(), held_as=jnp.bfloat16):
    result = spread * jax.random.normal(own_key, shape, jnp.float32)
    if shards:
        result = result * shard_levels(own_key, shape, shards, -0.22, 0.18)
    return jnp.clip(result, -reach, reach).astype(held_as)


def setup_inputs(seed: int = 0) -> dict:
    splits = jax.random.split(jax.random.key(seed), 6)
    return {
        "inputs": noise(splits[0], (TOKENS, D), 1.0, 6.0, ((0, 32), (1, 8))),
        "out_grad": noise(splits[1], (TOKENS, D), 1.0, 6.0, ((0, 32), (1, 8))),
        "pre_act": noise(splits[2], (TOKENS, FF), 1.0, 6.0, ((0, 8), (1, 32))),
        "w_up": noise(splits[3], (D, FF), D ** -0.5, 0.0546875, ((0, 8), (1, 32))),
        "w_down": noise(splits[4], (FF, D), FF ** -0.5, 0.0390625, ((0, 32), (1, 8))),
    }


def slope_and_act(pre):
    hval = pre.astype(jnp.float32)
    coeff = 0.7978845608028654
    inner = coeff * (hval + 0.044715 * hval * hval * hval)
    tanh_val = jnp.tanh(inner)
    slope = 0.5 * (1.0 + tanh_val) + 0.5 * hval * (1.0 - tanh_val * tanh_val) * coeff * (1.0 + 3.0 * 0.044715 * hval * hval)
    act = (0.5 * hval * (1.0 + tanh_val)).astype(jnp.bfloat16)
    return slope, act


def reference(inputs, out_grad, pre_act, w_up, w_down):
    scale = float(TOKENS) ** -0.5
    act_grad = lax.dot_general(out_grad, w_down, (((1,), (1,)), ((), ())), preferred_element_type=jnp.float32)
    slope, act = slope_and_act(pre_act)
    hidden_grad = (act_grad * slope).astype(jnp.bfloat16)
    input_grad = lax.dot_general(hidden_grad, w_up, (((1,), (1,)), ((), ())), preferred_element_type=jnp.float32).astype(jnp.bfloat16)
    up_grad = (lax.dot_general(inputs, hidden_grad, (((0,), (0,)), ((), ())), preferred_element_type=jnp.float32) * scale).astype(jnp.bfloat16)
    down_grad = (lax.dot_general(act, out_grad, (((0,), (0,)), ((), ())), preferred_element_type=jnp.float32) * scale).astype(jnp.bfloat16)
    return input_grad, up_grad, down_grad
```

```python
import functools

import jax
import jax.numpy as jnp
from jax import lax
from jax.experimental import pallas as pl
from jax.experimental.pallas import tpu as pltpu
from jax.sharding import PartitionSpec as P

MESH = pl.DeviceIdType.MESH
BF16 = jnp.bfloat16
F32 = jnp.float32
NT = (((1,), (1,)), ((), ()))
TN = (((0,), (0,)), ((), ()))
COLS = 16
ROWS = 8
TILE = 256


def kernel(
    H,
    in_ref, og_ref, pre_ref, wup_hbm, wdn_hbm,
    ig_out, up_hbm, dn_hbm,
    wup, wdn, slope, grads, ins, acts, part, rsr, hid, igs, igr, igf, igb, fin, up, dn,
    wsem, gs, gr, gfs, gfr, xs, xr, xfs, xfr, as_, ar, ps, pr, hs, hr, ss, sr, is_, ir, osem,
):
    R = 32 // H
    D = in_ref.shape[1]
    F = pre_ref.shape[1]
    row = lax.axis_index("row")
    col = lax.axis_index("col")
    chip = lax.div(col, 2)
    k = lax.rem(col, 2)
    y, xh = lax.div(row, 2), lax.rem(row, 2)
    xl, z = lax.div(chip, 8), lax.rem(chip, 8)

    def chip_at(o):
        return lax.rem(xl + lax.div(o, 8), 2) * 8 + lax.rem(z + o, 8)

    def col_dev(o):
        return (row, chip_at(o) * 2 + k)

    def row_at(o):
        return lax.rem(y + o, 4) * 2 + lax.rem(xh + lax.div(o, 4), 2)

    def row_dev(o):
        return (row_at(o), col)

    sib = (row, chip * 2 + 1 - k)

    def each(lo, hi, f):
        def body(o, carry):
            f(o)
            return carry
        lax.fori_loop(lo, hi, body, 0)

    def remote(src, dst, send, recv, dev):
        return pltpu.make_async_remote_copy(
            src_ref=src, dst_ref=dst, send_sem=send, recv_sem=recv, device_id=dev, device_id_type=MESH
        )

    wdn_copy = pltpu.make_async_copy(wdn_hbm, wdn, wsem.at[0])
    wup_copy = pltpu.make_async_copy(wup_hbm, wup, wsem.at[1])
    wdn_copy.start()
    wup_copy.start()

    barrier = pltpu.get_barrier_semaphore()
    each(1, COLS, lambda o: pl.semaphore_signal(barrier, inc=1, device_id=col_dev(o), device_id_type=MESH))
    each(1, ROWS, lambda o: pl.semaphore_signal(barrier, inc=1, device_id=row_dev(o), device_id_type=MESH))
    pl.semaphore_signal(barrier, inc=1, device_id=sib, device_id_type=MESH)
    pl.semaphore_wait(barrier, COLS + ROWS - 1)

    def c_grad(h, o):
        return remote(og_ref.at[pl.ds(h * R, R)], grads.at[chip, k, h], gs.at[h, o], gr.at[h, o], col_dev(o))

    def c_gradf(h):
        return remote(grads.at[:, k, h], grads.at[:, k, h], gfs.at[h], gfr.at[h], sib)

    def c_in(o):
        return remote(in_ref, ins.at[chip, k], xs.at[o], xr.at[o], col_dev(o))

    def c_inf():
        return remote(ins.at[:, k], ins.at[:, k], xfs, xfr, sib)

    def c_act(o):
        return remote(acts.at[pl.ds(2 * row, 2)], acts.at[pl.ds(2 * row, 2)], as_.at[o], ar.at[o], row_dev(o))

    def c_part(h, q, o):
        kk = k if q == 0 else 1 - k
        return remote(
            part.at[pl.ds(2 * row_at(o), 2), kk, h], rsr.at[o, :, kk, h], ps.at[h, q, o], pr.at[h, q, o], row_dev(o)
        )

    def c_hid(h, o):
        block = hid.at[pl.ds(2 * row, 2), :, h]
        return remote(block, block, hs.at[h, o], hr.at[h, o], row_dev(o))

    def c_igs(h):
        return remote(igs.at[h], igr.at[h], ss.at[h], sr.at[h], sib)

    def c_ig(h, o):
        return remote(igb.at[h, chip_at(o)], fin.at[o, h], is_.at[h, o], ir.at[h, o], col_dev(o))

    for h in range(H):
        each(1, COLS, lambda o: c_grad(h, o).start())
        grads[chip, k, h] = og_ref[h * R:(h + 1) * R]
    ins[chip, k] = in_ref[...]

    def gelu(b):
        hval = pre_ref[pl.ds(b * 32, 32), :].astype(F32)
        coeff = 0.7978845608028654
        inner = coeff * (hval + 0.044715 * hval * hval * hval)
        t = jnp.tanh(inner)
        act = (0.5 * hval * (1.0 + t)).astype(BF16)
        acts[2 * row + lax.div(b, 2), lax.rem(b, 2)] = act
        sl = 0.5 * (1.0 + t) + 0.5 * hval * (1.0 - t * t) * coeff * (1.0 + 3.0 * 0.044715 * hval * hval)
        for h in range(H):
            slope[lax.div(b, 2), lax.rem(b, 2), h] = sl[h * R:(h + 1) * R]

    each(0, 4, gelu)
    each(1, ROWS, lambda o: c_act(o).start())

    def mm1(h, kk):
        def tile(n):
            cols = pl.ds(pl.multiple_of(n * TILE, TILE), TILE)
            lhs = grads[:, kk, h].reshape(16 * R, D)
            acc = lax.dot_general(lhs, wdn[cols, :], NT, preferred_element_type=F32)
            part[:, kk, h, :, cols] = acc.astype(BF16).reshape(16, R, TILE)
        each(0, F // TILE, tile)

    wdn_copy.wait()
    for h in range(H):
        each(1, COLS, lambda o: c_grad(h, o).wait_recv())
        c_gradf(h).start()
        mm1(h, k)
        each(1, ROWS, lambda o: c_part(h, 0, o).start())
        c_gradf(h).wait_recv()
        mm1(h, 1 - k)
        each(1, ROWS, lambda o: c_part(h, 1, o).start())

    each(1, COLS, lambda o: c_in(o).start())

    scale = 0.03125

    def c_dn(m):
        rows = pl.ds(m * TILE, TILE)
        return pltpu.make_async_copy(dn.at[rows], dn_hbm.at[rows], osem.at[m])

    def mm_dn(m):
        cols = pl.ds(pl.multiple_of(m * TILE, TILE), TILE)
        lhs = acts[:, :, :, cols].reshape(1024, TILE)
        def half(n):
            oc = pl.ds(pl.multiple_of(n * 512, 512), 512)
            rhs = grads[:, :, :, :, oc].reshape(1024, 512)
            acc = lax.dot_general(lhs, rhs, TN, preferred_element_type=F32)
            dn[pl.ds(m * TILE, TILE), oc] = (acc * scale).astype(BF16)
        each(0, D // 512, half)
        c_dn(m).start()

    def hidden(h):
        each(1, ROWS, lambda o: c_part(h, 0, o).wait_recv())
        each(1, ROWS, lambda o: c_part(h, 1, o).wait_recv())

        def block(b):
            zz, kk = lax.div(b, 2), lax.rem(b, 2)
            acc = part[2 * row + zz, kk, h].astype(F32)
            for o in range(1, ROWS):
                acc += rsr[o, zz, kk, h].astype(F32)
            hid[2 * row + zz, kk, h] = (acc * slope[zz, kk, h]).astype(BF16)

        each(0, 4, block)
        each(1, ROWS, lambda o: c_hid(h, o).start())

    for h in range(H):
        hidden(h)

    each(1, ROWS, lambda o: c_act(o).wait_recv())
    each(0, F // TILE, mm_dn)

    def mm_ig(h, kk, put):
        def tile(n):
            cols = pl.ds(pl.multiple_of(n * TILE, TILE), TILE)
            lhs = hid[:, kk, h].reshape(16 * R, F)
            acc = lax.dot_general(lhs, wup[cols, :], NT, preferred_element_type=F32)
            put(cols, acc.reshape(16, R, TILE))
        each(0, D // TILE, tile)

    def put_sib(h):
        def put(cols, acc):
            igs[h, :, :, cols] = acc.astype(BF16)
        return put

    def put_own(cols, acc):
        igf[:, :, cols] = acc

    wup_copy.wait()
    for h in range(H):
        each(1, ROWS, lambda o: c_hid(h, o).wait_recv())
        mm_ig(h, 1 - k, put_sib(h))
        c_igs(h).start()
        mm_ig(h, k, put_own)
        c_igs(h).wait_recv()

        def add(j):
            igb[h, j] = (igf[j] + igr[h, j].astype(F32)).astype(BF16)

        each(0, COLS, add)
        each(1, COLS, lambda o: c_ig(h, o).start())

    each(1, COLS, lambda o: c_in(o).wait_recv())
    c_inf().start()
    c_inf().wait_recv()

    def c_up(m):
        rows = pl.ds(m * TILE, TILE)
        return pltpu.make_async_copy(up.at[rows], up_hbm.at[rows], osem.at[F // TILE + m])

    def mm_up(m):
        cols = pl.ds(pl.multiple_of(m * TILE, TILE), TILE)
        lhs = ins[:, :, :, cols].reshape(1024, TILE)
        rhs = hid[...].reshape(1024, F)
        acc = lax.dot_general(lhs, rhs, TN, preferred_element_type=F32)
        up[pl.ds(m * TILE, TILE), :] = (acc * scale).astype(BF16)
        c_up(m).start()

    each(0, D // TILE, mm_up)

    for h in range(H):
        each(1, COLS, lambda o: c_ig(h, o).wait_recv())

        def total(n):
            cols = pl.ds(pl.multiple_of(n * 512, 512), 512)
            acc = igb[h, chip, :, cols].astype(F32)
            for o in range(1, COLS):
                acc += fin[o, h, :, cols].astype(F32)
            ig_out[pl.ds(h * R, R), cols] = acc.astype(BF16)

        each(0, D // 512, total)

    for h in range(H):
        each(1, COLS, lambda o: c_grad(h, o).wait_send())
        c_gradf(h).wait_send()
        for q in range(2):
            each(1, ROWS, lambda o: c_part(h, q, o).wait_send())
        each(1, ROWS, lambda o: c_hid(h, o).wait_send())
        c_igs(h).wait_send()
        each(1, COLS, lambda o: c_ig(h, o).wait_send())
    each(1, COLS, lambda o: c_in(o).wait_send())
    c_inf().wait_send()
    each(1, ROWS, lambda o: c_act(o).wait_send())
    each(0, F // TILE, lambda m: c_dn(m).wait())
    each(0, D // TILE, lambda m: c_up(m).wait())


def per_device(H, inputs, out_grad, pre_act, w_up, w_down):
    R = 32 // H
    D = inputs.shape[1]
    F = pre_act.shape[1]
    vmem = pl.BlockSpec(memory_space=pltpu.VMEM)
    hbm = pl.BlockSpec(memory_space=pl.ANY)
    dma = pltpu.SemaphoreType.DMA
    return pl.pallas_call(
        functools.partial(kernel, H),
        out_shape=(
            jax.ShapeDtypeStruct((32, D), BF16),
            jax.ShapeDtypeStruct((D, F), BF16),
            jax.ShapeDtypeStruct((F, D), BF16),
        ),
        in_specs=[vmem, vmem, vmem, hbm, hbm],
        out_specs=(vmem, hbm, hbm),
        scratch_shapes=[
            pltpu.VMEM((D, F), BF16),
            pltpu.VMEM((F, D), BF16),
            pltpu.VMEM((2, 2, H, R, F), F32),
            pltpu.VMEM((COLS, 2, H, R, D), BF16),
            pltpu.VMEM((COLS, 2, 32, D), BF16),
            pltpu.VMEM((COLS, 2, 32, F), BF16),
            pltpu.VMEM((COLS, 2, H, R, F), BF16),
            pltpu.VMEM((ROWS, 2, 2, H, R, F), BF16),
            pltpu.VMEM((COLS, 2, H, R, F), BF16),
            pltpu.VMEM((H, COLS, R, D), BF16),
            pltpu.VMEM((H, COLS, R, D), BF16),
            pltpu.VMEM((COLS, R, D), F32),
            pltpu.VMEM((H, COLS, R, D), BF16),
            pltpu.VMEM((COLS, H, R, D), BF16),
            pltpu.VMEM((D, F), BF16),
            pltpu.VMEM((F, D), BF16),
            dma((2,)),
            dma((H, COLS)), dma((H, COLS)), dma((H,)), dma((H,)),
            dma((COLS,)), dma((COLS,)), dma, dma,
            dma((ROWS,)), dma((ROWS,)),
            dma((H, 2, ROWS)), dma((H, 2, ROWS)),
            dma((H, ROWS)), dma((H, ROWS)),
            dma((H,)), dma((H,)),
            dma((H, COLS)), dma((H, COLS)),
            dma((F // TILE + D // TILE,)),
        ],
        compiler_params=pltpu.CompilerParams(
            collective_id=0, has_side_effects=True, vmem_limit_bytes=56 * 2**20
        ),
        cost_estimate=pl.CostEstimate(flops=8 * 1024 * 1536 * 768, bytes_accessed=10 * 2**20, transcendentals=128 * 768),
    )(inputs, out_grad, pre_act, w_up, w_down)


def solution(mesh):
    return jax.shard_map(
        functools.partial(per_device, 2),
        mesh=mesh,
        in_specs=(P("col", "row"), P("col", "row"), P("row", "col"), P("row", "col"), P("col", "row")),
        out_specs=(P("col", "row"), P("row", "col"), P("col", "row")),
        check_vma=False,
    )
```

```python
import functools

import jax
import jax.numpy as jnp
from jax import lax
from jax.experimental import pallas as pl
from jax.experimental.pallas import tpu as pltpu
from jax.sharding import PartitionSpec as P

MESH = pl.DeviceIdType.MESH
BF16 = jnp.bfloat16
F32 = jnp.float32
NT = (((1,), (1,)), ((), ()))
TN = (((0,), (0,)), ((), ()))
COLS = 16
ROWS = 8
TILE = 256


def kernel(
    H,
    in_ref, og_ref, pre_ref, wup_hbm, wdn_hbm,
    ig_out, up_hbm, dn_hbm,
    wup, wdn, slope, grads, ins, acts, part, rsr, hid, igs, igr, igf, igb, igx, igz, igo, fin, up, dn,
    wsem, gxs, gxr, gs, gr, gfs, gfr, xxs, xxr, xs, xr, xfs, xfr, as_, ar, ps, pr, hs, hr, ss, sr,
    bxs, bxr, is_, ir, osem,
):
    R = 32 // H
    D = in_ref.shape[1]
    F = pre_ref.shape[1]
    row = lax.axis_index("row")
    col = lax.axis_index("col")
    chip = lax.div(col, 2)
    k = lax.rem(col, 2)
    y, xh = lax.div(row, 2), lax.rem(row, 2)
    xl, z = lax.div(chip, 8), lax.rem(chip, 8)

    def z_at(dz):
        return lax.rem(z + dz, 8)

    def z_dev(dz):
        return (row, (xl * 8 + z_at(dz)) * 2 + k)

    other = (1 - xl) * 8
    partner = (row, (other + z) * 2 + k)

    def row_at(o):
        return lax.rem(y + o, 4) * 2 + lax.rem(xh + lax.div(o, 4), 2)

    def row_dev(o):
        return (row_at(o), col)

    sib = (row, chip * 2 + 1 - k)

    def each(lo, hi, f):
        def body(o, carry):
            f(o)
            return carry
        lax.fori_loop(lo, hi, body, 0)

    def remote(src, dst, send, recv, dev):
        return pltpu.make_async_remote_copy(
            src_ref=src, dst_ref=dst, send_sem=send, recv_sem=recv, device_id=dev, device_id_type=MESH
        )

    wdn_copy = pltpu.make_async_copy(wdn_hbm, wdn, wsem.at[0])
    wup_copy = pltpu.make_async_copy(wup_hbm, wup, wsem.at[1])
    wdn_copy.start()
    wup_copy.start()

    barrier = pltpu.get_barrier_semaphore()
    each(1, 8, lambda o: pl.semaphore_signal(barrier, inc=1, device_id=z_dev(o), device_id_type=MESH))
    pl.semaphore_signal(barrier, inc=1, device_id=partner, device_id_type=MESH)
    each(1, ROWS, lambda o: pl.semaphore_signal(barrier, inc=1, device_id=row_dev(o), device_id_type=MESH))
    pl.semaphore_signal(barrier, inc=1, device_id=sib, device_id_type=MESH)
    pl.semaphore_wait(barrier, 7 + 1 + 1 + ROWS - 1)

    def ring_block(p, d, s):
        return (xl * 8 if p == 0 else other) + z_at((9 - s) % 8 if d == 0 else s - 1)

    def ring_ok(p, d, s):
        return s < 4 or (s == 4 and p == d)

    def c_gradx(h):
        return remote(grads.at[chip, k, h], grads.at[chip, k, h], gxs.at[h], gxr.at[h], partner)

    def c_grad(h, p, d, s):
        block = grads.at[ring_block(p, d, s), k, h]
        i = (p * 2 + d) * 4 + s - 1
        return remote(block, block, gs.at[h, i], gr.at[h, i], z_dev(1 if d == 0 else 7))

    def c_inx():
        return remote(ins.at[chip, k], ins.at[chip, k], xxs, xxr, partner)

    def c_in(p, d, s):
        block = ins.at[ring_block(p, d, s), k]
        i = (p * 2 + d) * 4 + s - 1
        return remote(block, block, xs.at[i], xr.at[i], z_dev(1 if d == 0 else 7))

    def c_gradf(h):
        return remote(grads.at[:, k, h], grads.at[:, k, h], gfs.at[h], gfr.at[h], sib)

    def c_inf():
        return remote(ins.at[:, k], ins.at[:, k], xfs, xfr, sib)

    def c_act(o):
        return remote(acts.at[pl.ds(2 * row, 2)], acts.at[pl.ds(2 * row, 2)], as_.at[o], ar.at[o], row_dev(o))

    def c_part(h, q, o):
        kk = k if q == 0 else 1 - k
        return remote(
            part.at[pl.ds(2 * row_at(o), 2), kk, h], rsr.at[o, :, kk, h], ps.at[h, q, o], pr.at[h, q, o], row_dev(o)
        )

    def c_hid(h, o):
        block = hid.at[pl.ds(2 * row, 2), :, h]
        return remote(block, block, hs.at[h, o], hr.at[h, o], row_dev(o))

    def c_igs(h, c):
        return remote(igs.at[h, c, :, 1 - k], igr.at[h, c], ss.at[h, c], sr.at[h, c], sib)

    def c_igx(h, o):
        return remote(igb.at[h, z_at(o)], igx.at[h, z_at(o)], bxs.at[h, o], bxr.at[h, o], partner)

    def c_ig(h, o):
        return remote(igz.at[h, z_at(o)], fin.at[o, h], is_.at[h, o], ir.at[h, o], z_dev(o))

    for h in range(H):
        grads[chip, k, h] = og_ref[h * R:(h + 1) * R]
        for d in range(2):
            c_grad(h, 0, d, 1).start()
        c_gradx(h).start()
    ins[chip, k] = in_ref[...]

    def gelu(b):
        hval = pre_ref[pl.ds(b * 32, 32), :].astype(F32)
        coeff = 0.7978845608028654
        inner = coeff * (hval + 0.044715 * hval * hval * hval)
        t = jnp.tanh(inner)
        act = (0.5 * hval * (1.0 + t)).astype(BF16)
        acts[2 * row + lax.div(b, 2), lax.rem(b, 2)] = act
        sl = 0.5 * (1.0 + t) + 0.5 * hval * (1.0 - t * t) * coeff * (1.0 + 3.0 * 0.044715 * hval * hval)
        for h in range(H):
            slope[lax.div(b, 2), lax.rem(b, 2), h] = sl[h * R:(h + 1) * R]

    each(0, 4, gelu)
    each(1, ROWS, lambda o: c_act(o).start())

    def mm1(h, kk):
        def tile(n):
            cols = pl.ds(pl.multiple_of(n * TILE, TILE), TILE)
            lhs = grads[:, kk, h].reshape(16 * R, D)
            acc = lax.dot_general(lhs, wdn[cols, :], NT, preferred_element_type=F32)
            part[:, kk, h, :, cols] = acc.astype(BF16).reshape(16, R, TILE)
        each(0, F // TILE, tile)

    for h in range(H):
        c_gradx(h).wait_recv()
        for d in range(2):
            c_grad(h, 1, d, 1).start()
    def grad_step(h, s):
        for p in range(2):
            for d in range(2):
                if ring_ok(p, d, s):
                    c_grad(h, p, d, s).wait_recv()
                    if ring_ok(p, d, s + 1):
                        c_grad(h, p, d, s + 1).start()

    for s in range(1, 4):
        for h in range(H):
            grad_step(h, s)

    for h in range(H):
        grad_step(h, 4)
        c_gradf(h).start()
        if h == H - 1:
            c_inx().start()
            for d in range(2):
                c_in(0, d, 1).start()
        if h == 0:
            wdn_copy.wait()
        mm1(h, k)
        each(1, ROWS, lambda o: c_part(h, 0, o).start())
        c_gradf(h).wait_recv()
        mm1(h, 1 - k)
        each(1, ROWS, lambda o: c_part(h, 1, o).start())

    def in_step(s):
        for p in range(2):
            for d in range(2):
                if ring_ok(p, d, s):
                    c_in(p, d, s).wait_recv()
                    if ring_ok(p, d, s + 1):
                        c_in(p, d, s + 1).start()

    scale = 0.03125

    def c_dn(m):
        rows = pl.ds(m * TILE, TILE)
        return pltpu.make_async_copy(dn.at[rows], dn_hbm.at[rows], osem.at[m])

    def mm_dn(m):
        cols = pl.ds(pl.multiple_of(m * TILE, TILE), TILE)
        lhs = acts[:, :, :, cols].reshape(1024, TILE)
        def half(n):
            oc = pl.ds(pl.multiple_of(n * 512, 512), 512)
            rhs = grads[:, :, :, :, oc].reshape(1024, 512)
            acc = lax.dot_general(lhs, rhs, TN, preferred_element_type=F32)
            dn[pl.ds(m * TILE, TILE), oc] = (acc * scale).astype(BF16)
        each(0, D // 512, half)
        c_dn(m).start()

    def hidden(h):
        each(1, ROWS, lambda o: c_part(h, 0, o).wait_recv())
        each(1, ROWS, lambda o: c_part(h, 1, o).wait_recv())

        def block(b):
            zz, kk = lax.div(b, 2), lax.rem(b, 2)
            acc = part[2 * row + zz, kk, h].astype(F32)
            for o in range(1, ROWS):
                acc += rsr[o, zz, kk, h].astype(F32)
            hid[2 * row + zz, kk, h] = (acc * slope[zz, kk, h]).astype(BF16)

        each(0, 4, block)
        each(1, ROWS, lambda o: c_hid(h, o).start())

    each(1, ROWS, lambda o: c_act(o).wait_recv())
    c_inx().wait_recv()
    for d in range(2):
        c_in(1, d, 1).start()
    if H == 1:
        in_step(1)
        mm_dn(0)
        hidden(0)
        in_step(2)
        mm_dn(1)
        in_step(3)
        mm_dn(2)
        in_step(4)
    else:
        in_step(1)
        hidden(0)
        mm_dn(0)
        in_step(2)
        hidden(1)
        mm_dn(1)
        in_step(3)
        mm_dn(2)

    def mm_ig(h, c):
        first = other if c == 0 else xl * 8
        def tile(n):
            cols = pl.ds(pl.multiple_of(n * TILE, TILE), TILE)
            lhs = hid[pl.ds(first, 8), :, h].reshape(16 * R, F)
            acc = lax.dot_general(lhs, wup[cols, :], NT, preferred_element_type=F32).reshape(8, 2, R, TILE)
            igf[h, c, :, :, :, cols] = acc
            igs[h, c, :, :, :, cols] = acc.astype(BF16)
        each(0, D // TILE, tile)

    def share(h, o):
        j = z_at(o)
        igb[h, j] = (igf[h, 0, j, k] + igr[h, 0, j].astype(F32)).astype(BF16)
        c_igx(h, o).start()

    def pass_on(h, o):
        j = z_at(o)
        c_igx(h, o).wait_recv()
        acc = igf[h, 1, j, k] + igr[h, 1, j].astype(F32) + igx[h, j].astype(F32)
        if o == 0:
            igo[h] = acc
        else:
            igz[h, j] = acc.astype(BF16)
            c_ig(h, o).start()

    order = (4, 3, 5, 2, 6, 1, 7, 0)

    def ig(h):
        each(1, ROWS, lambda o: c_hid(h, o).wait_recv())
        mm_ig(h, 0)
        c_igs(h, 0).start()
        mm_ig(h, 1)
        c_igs(h, 1).start()
        c_igs(h, 0).wait_recv()
        for o in order:
            share(h, o)
        if h == 0:
            if H == 2:
                in_step(4)
            c_inf().start()
        c_igs(h, 1).wait_recv()

    wup_copy.wait()
    ig(0)
    if H == 2:
        for o in order[:4]:
            pass_on(0, o)
        ig(1)
        for o in order[4:]:
            pass_on(0, o)
    for o in order:
        pass_on(H - 1, o)

    c_inf().wait_recv()

    def c_up(m):
        rows = pl.ds(m * TILE, TILE)
        return pltpu.make_async_copy(up.at[rows], up_hbm.at[rows], osem.at[F // TILE + m])

    def mm_up(m):
        cols = pl.ds(pl.multiple_of(m * TILE, TILE), TILE)
        lhs = ins[:, :, :, cols].reshape(1024, TILE)
        rhs = hid[...].reshape(1024, F)
        acc = lax.dot_general(lhs, rhs, TN, preferred_element_type=F32)
        up[pl.ds(m * TILE, TILE), :] = (acc * scale).astype(BF16)
        c_up(m).start()

    each(0, D // TILE, mm_up)

    for h in range(H):
        each(1, 8, lambda o: c_ig(h, o).wait_recv())

        def total(n):
            cols = pl.ds(pl.multiple_of(n * 512, 512), 512)
            acc = igo[h, :, cols]
            for o in range(1, 8):
                acc += fin[o, h, :, cols].astype(F32)
            ig_out[pl.ds(h * R, R), cols] = acc.astype(BF16)

        each(0, D // 512, total)

    for p in range(2):
        for d in range(2):
            for t in range(1, 5):
                if ring_ok(p, d, t):
                    for h in range(H):
                        c_grad(h, p, d, t).wait_send()
                    c_in(p, d, t).wait_send()
    for h in range(H):
        c_gradx(h).wait_send()
        c_gradf(h).wait_send()
        for q in range(2):
            each(1, ROWS, lambda o: c_part(h, q, o).wait_send())
        each(1, ROWS, lambda o: c_hid(h, o).wait_send())
        for c in range(2):
            c_igs(h, c).wait_send()
        each(0, 8, lambda o: c_igx(h, o).wait_send())
        each(1, 8, lambda o: c_ig(h, o).wait_send())
    c_inx().wait_send()
    c_inf().wait_send()
    each(1, ROWS, lambda o: c_act(o).wait_send())
    each(0, F // TILE, lambda m: c_dn(m).wait())
    each(0, D // TILE, lambda m: c_up(m).wait())


def copy_kernel(ig, up, dn, ig_out, up_out, dn_out, ig_v, up_v, dn_v, sem):
    steps = [(ig, ig_v, ig_out, pl.ds(0, ig.shape[0]))]
    for src, buf, dst in ((up, up_v, up_out), (dn, dn_v, dn_out)):
        n = src.shape[0] // 4
        steps += [(src, buf, dst, pl.ds(i * n, n)) for i in range(4)]
    loads = [pltpu.make_async_copy(s.at[r], v.at[r], sem.at[0, i]) for i, (s, v, d, r) in enumerate(steps)]
    stores = [pltpu.make_async_copy(v.at[r], d.at[r], sem.at[1, i]) for i, (s, v, d, r) in enumerate(steps)]
    for copy in loads:
        copy.start()
    for load, store in zip(loads, stores):
        load.wait()
        store.start()
    for copy in stores:
        copy.wait()


def per_device(H, inputs, out_grad, pre_act, w_up, w_down):
    R = 32 // H
    D = inputs.shape[1]
    F = pre_act.shape[1]
    vmem = pl.BlockSpec(memory_space=pltpu.VMEM)
    hbm = pl.BlockSpec(memory_space=pl.ANY)
    dma = pltpu.SemaphoreType.DMA
    shapes = (
        jax.ShapeDtypeStruct((32, D), BF16),
        jax.ShapeDtypeStruct((D, F), BF16),
        jax.ShapeDtypeStruct((F, D), BF16),
    )
    results = pl.pallas_call(
        functools.partial(kernel, H),
        out_shape=shapes,
        in_specs=[vmem, vmem, vmem, hbm, hbm],
        out_specs=(vmem, hbm, hbm),
        scratch_shapes=[
            pltpu.VMEM((D, F), BF16),
            pltpu.VMEM((F, D), BF16),
            pltpu.VMEM((2, 2, H, R, F), F32),
            pltpu.VMEM((COLS, 2, H, R, D), BF16),
            pltpu.VMEM((COLS, 2, 32, D), BF16),
            pltpu.VMEM((COLS, 2, 32, F), BF16),
            pltpu.VMEM((COLS, 2, H, R, F), BF16),
            pltpu.VMEM((ROWS, 2, 2, H, R, F), BF16),
            pltpu.VMEM((COLS, 2, H, R, F), BF16),
            pltpu.VMEM((H, 2, 8, 2, R, D), BF16),
            pltpu.VMEM((H, 2, 8, R, D), BF16),
            pltpu.VMEM((H, 2, 8, 2, R, D), F32),
            pltpu.VMEM((H, 8, R, D), BF16),
            pltpu.VMEM((H, 8, R, D), BF16),
            pltpu.VMEM((H, 8, R, D), BF16),
            pltpu.VMEM((H, R, D), F32),
            pltpu.VMEM((8, H, R, D), BF16),
            pltpu.VMEM((D, F), BF16),
            pltpu.VMEM((F, D), BF16),
            dma((2,)),
            dma((H,)), dma((H,)),
            dma((H, 16)), dma((H, 16)), dma((H,)), dma((H,)),
            dma, dma,
            dma((16,)), dma((16,)), dma, dma,
            dma((ROWS,)), dma((ROWS,)),
            dma((H, 2, ROWS)), dma((H, 2, ROWS)),
            dma((H, ROWS)), dma((H, ROWS)),
            dma((H, 2)), dma((H, 2)),
            dma((H, 8)), dma((H, 8)),
            dma((H, 8)), dma((H, 8)),
            dma((F // TILE + D // TILE,)),
        ],
        compiler_params=pltpu.CompilerParams(
            collective_id=0, has_side_effects=True, vmem_limit_bytes=56 * 2**20
        ),
        cost_estimate=pl.CostEstimate(flops=8 * 1024 * 1536 * 768, bytes_accessed=10 * 2**20, transcendentals=128 * 768),
    )(inputs, out_grad, pre_act, w_up, w_down)
    return pl.pallas_call(
        copy_kernel,
        out_shape=shapes,
        in_specs=[hbm] * 3,
        out_specs=(hbm,) * 3,
        scratch_shapes=[pltpu.VMEM(r.shape, BF16) for r in shapes] + [dma((2, 9))],
        compiler_params=pltpu.CompilerParams(vmem_limit_bytes=56 * 2**20),
    )(*results)


def solution(mesh):
    return jax.shard_map(
        functools.partial(per_device, 2),
        mesh=mesh,
        in_specs=(P("col", "row"), P("col", "row"), P("row", "col"), P("row", "col"), P("col", "row")),
        out_specs=(P("col", "row"), P("row", "col"), P("col", "row")),
        check_vma=False,
    )
```

```python
import functools

import jax
import jax.numpy as jnp
from jax import lax
from jax.experimental import pallas as pl
from jax.experimental.pallas import tpu as pltpu
from jax.sharding import PartitionSpec as P

MESH = pl.DeviceIdType.MESH
BF16 = jnp.bfloat16
F32 = jnp.float32
NT = (((1,), (1,)), ((), ()))
TN = (((0,), (0,)), ((), ()))
COLS = 16
ROWS = 8
TILE = 256


def kernel(
    H,
    in_ref, og_ref, pre_ref, wup_hbm, wdn_hbm,
    ig_out, up_hbm, dn_hbm,
    wup, wdn, slope, grads, ins, acts, part, prx, p2s, p2r, q1r, q2s, q2r, hid, igs, igr, igf, igb, igx, igz, igo, fin, up, dn,
    wsem, gxs, gxr, gs, gr, gfs, gfr, xxs, xxr, xs, xr, xfs, xfr, as_, ar, pxs, pxr, p2ss, p2rs, q1ss, q1rs, q2ss, q2rs, hs, hr, hxs, hxr, ss, sr,
    bxs, bxr, is_, ir, osem,
):
    R = 32 // H
    D = in_ref.shape[1]
    F = pre_ref.shape[1]
    row = lax.axis_index("row")
    col = lax.axis_index("col")
    chip = lax.div(col, 2)
    k = lax.rem(col, 2)
    y, xh = lax.div(row, 2), lax.rem(row, 2)
    xl, z = lax.div(chip, 8), lax.rem(chip, 8)

    def z_at(dz):
        return lax.rem(z + dz, 8)

    def z_dev(dz):
        return (row, (xl * 8 + z_at(dz)) * 2 + k)

    other = (1 - xl) * 8
    partner = (row, (other + z) * 2 + k)

    def row_at(o):
        return lax.rem(y + o, 4) * 2 + lax.rem(xh + lax.div(o, 4), 2)

    def row_dev(o):
        return (row_at(o), col)

    def y_at(dy):
        return lax.rem(y + dy, 4)

    def y_dev(dy):
        return (y_at(dy) * 2 + xh, col)

    across = (y * 2 + 1 - xh, col)
    sib = (row, chip * 2 + 1 - k)

    def each(lo, hi, f):
        def body(o, carry):
            f(o)
            return carry
        lax.fori_loop(lo, hi, body, 0)

    def remote(src, dst, send, recv, dev):
        return pltpu.make_async_remote_copy(
            src_ref=src, dst_ref=dst, send_sem=send, recv_sem=recv, device_id=dev, device_id_type=MESH
        )

    wdn_copy = pltpu.make_async_copy(wdn_hbm, wdn, wsem.at[0])
    wup_copy = pltpu.make_async_copy(wup_hbm, wup, wsem.at[1])
    wdn_copy.start()
    wup_copy.start()

    barrier = pltpu.get_barrier_semaphore()
    each(1, 8, lambda o: pl.semaphore_signal(barrier, inc=1, device_id=z_dev(o), device_id_type=MESH))
    pl.semaphore_signal(barrier, inc=1, device_id=partner, device_id_type=MESH)
    each(1, ROWS, lambda o: pl.semaphore_signal(barrier, inc=1, device_id=row_dev(o), device_id_type=MESH))
    pl.semaphore_signal(barrier, inc=1, device_id=sib, device_id_type=MESH)
    pl.semaphore_wait(barrier, 7 + 1 + 1 + ROWS - 1)

    RING = {1: (0, 1), 2: (1, 1), 3: (2, 1), 4: (3, 1)}
    FAST = {1: (0, 1), 2: (0, 2), 3: (2, 1), 4: (2, 2)}

    def ring_block(way, p, d, s):
        back = way[s][0]
        return (xl * 8 if p == 0 else other) + z_at((8 - back) % 8 if d == 0 else back)

    def ring_dev(way, d, s):
        return z_dev(way[s][1] if d == 0 else 8 - way[s][1])

    def ring_ok(p, d, s):
        return s < 4 or (s == 4 and p == d)

    def grad_way(h):
        return FAST if H == 2 and h == 0 else RING

    def c_gradx(h):
        return remote(grads.at[chip, k, h], grads.at[chip, k, h], gxs.at[h], gxr.at[h], partner)

    def c_grad(h, p, d, s):
        block = grads.at[ring_block(grad_way(h), p, d, s), k, h]
        i = (p * 2 + d) * 4 + s - 1
        return remote(block, block, gs.at[h, i], gr.at[h, i], ring_dev(grad_way(h), d, s))

    def c_inx():
        return remote(ins.at[chip, k], ins.at[chip, k], xxs, xxr, partner)

    def c_in(p, d, s):
        block = ins.at[ring_block(RING, p, d, s), k]
        i = (p * 2 + d) * 4 + s - 1
        return remote(block, block, xs.at[i], xr.at[i], ring_dev(RING, d, s))

    def c_gradf(h):
        return remote(grads.at[:, k, h], grads.at[:, k, h], gfs.at[h], gfr.at[h], sib)

    def c_inf():
        return remote(ins.at[:, k], ins.at[:, k], xfs, xfr, sib)

    def c_act(o):
        return remote(acts.at[pl.ds(2 * row, 2)], acts.at[pl.ds(2 * row, 2)], as_.at[o], ar.at[o], row_dev(o))

    def c_px(h):
        return remote(part.at[:, 1 - xh, :, k, h], prx.at[h], pxs.at[h], pxr.at[h], across)

    def c_p2(h, dy):
        return remote(p2s.at[h, dy], p2r.at[h, dy], p2ss.at[h, dy], p2rs.at[h, dy], y_dev(dy))

    def c_q1(h, dy):
        return remote(part.at[y_at(dy), :, :, 1 - k, h], q1r.at[h, dy], q1ss.at[h, dy], q1rs.at[h, dy], y_dev(dy))

    def c_q2(h):
        return remote(q2s.at[h], q2r.at[h], q2ss.at[h], q2rs.at[h], across)

    def c_hid(h, i, dy):
        if i == 0:
            block, dev = hid.at[y, xh, :, :, h], y_dev(dy)
        elif i == 1:
            block, dev = hid.at[y, 1 - xh, :, 0, h], y_dev(dy)
        else:
            block, dev = hid.at[y_at(4 - dy), xh, :, 1, h], across
        return remote(block, block, hs.at[h, i, dy], hr.at[h, i, dy], dev)

    def c_hidx(h):
        block = hid.at[y, xh, :, :, h]
        return remote(block, block, hxs.at[h], hxr.at[h], across)

    def c_igs(h, c):
        return remote(igs.at[h, c, :, 1 - k], igr.at[h, c], ss.at[h, c], sr.at[h, c], sib)

    def c_igx(h, o):
        return remote(igb.at[h, z_at(o)], igx.at[h, z_at(o)], bxs.at[h, o], bxr.at[h, o], partner)

    def c_ig(h, o):
        return remote(igz.at[h, z_at(o)], fin.at[o, h], is_.at[h, o], ir.at[h, o], z_dev(o))

    def grad_first(h, p):
        for s in (1, 2) if grad_way(h) is FAST else (1,):
            for d in range(2):
                c_grad(h, p, d, s).start()

    for h in range(H):
        grads[chip, k, h] = og_ref[h * R:(h + 1) * R]
        c_gradx(h).start()
        grad_first(h, 0)
    ins[chip, k] = in_ref[...]

    def gelu(b):
        hval = pre_ref[pl.ds(b * 32, 32), :].astype(F32)
        coeff = 0.7978845608028654
        inner = coeff * (hval + 0.044715 * hval * hval * hval)
        t = jnp.tanh(inner)
        act = (0.5 * hval * (1.0 + t)).astype(BF16)
        acts[2 * row + lax.div(b, 2), lax.rem(b, 2)] = act
        sl = 0.5 * (1.0 + t) + 0.5 * hval * (1.0 - t * t) * coeff * (1.0 + 3.0 * 0.044715 * hval * hval)
        for h in range(H):
            slope[lax.div(b, 2), lax.rem(b, 2), h] = sl[h * R:(h + 1) * R]

    each(0, 4, gelu)
    each(1, ROWS, lambda o: c_act(o).start())

    def mm1(h, kk):
        def tile(n):
            cols = pl.ds(pl.multiple_of(n * TILE, TILE), TILE)
            lhs = grads[:, kk, h].reshape(16 * R, D)
            acc = lax.dot_general(lhs, wdn[cols, :], NT, preferred_element_type=F32)
            part[:, :, :, kk, h, :, cols] = acc.astype(BF16).reshape(4, 2, 2, R, TILE)
        each(0, F // TILE, tile)

    def grad_step(h, s):
        for p in range(2):
            for d in range(2):
                if ring_ok(p, d, s):
                    c_grad(h, p, d, s).wait_recv()
                    if ring_ok(p, d, s + 1):
                        c_grad(h, p, d, s + 1).start()

    def mm1_own(h):
        c_gradf(h).start()
        if h == 0:
            wdn_copy.wait()
        mm1(h, k)
        c_px(h).start()

    def mm1_sib(h):
        c_gradf(h).wait_recv()
        mm1(h, 1 - k)
        each(1, 4, lambda dy: c_q1(h, dy).start())

    def add_p(h):
        c_px(h).wait_recv()

        def one(dy):
            yy = y_at(dy)
            p2s[h, dy] = (part[yy, xh, :, k, h].astype(F32) + prx[h, yy].astype(F32)).astype(BF16)
            c_p2(h, dy).start()

        each(1, 4, one)

    def add_q(h):
        each(1, 4, lambda dy: c_q1(h, dy).wait_recv())
        acc = part[y, 1 - xh, :, 1 - k, h].astype(F32)
        for dy in range(1, 4):
            acc += q1r[h, dy, 1 - xh].astype(F32)
        q2s[h] = acc.astype(BF16)
        c_q2(h).start()

    def in_first():
        c_inx().start()
        for d in range(2):
            c_in(0, d, 1).start()

    for h in range(H):
        c_gradx(h).wait_recv()
        grad_first(h, 1)
    if H == 1:
        for s in range(1, 5):
            grad_step(0, s)
        in_first()
        mm1_own(0)
        mm1_sib(0)
        add_p(0)
        add_q(0)
    else:
        for p in range(2):
            for d in range(2):
                c_grad(0, p, d, 2).wait_recv()
                for s in (3, 4):
                    if ring_ok(p, d, s):
                        c_grad(0, p, d, s).start()
        grad_step(1, 1)
        for s in (1, 3, 4):
            for p in range(2):
                for d in range(2):
                    if ring_ok(p, d, s):
                        c_grad(0, p, d, s).wait_recv()
        grad_step(1, 2)
        mm1_own(0)
        grad_step(1, 3)
        mm1_sib(0)
        grad_step(1, 4)
        mm1_own(1)
        in_first()
        add_p(0)
        mm1_sib(1)
        add_q(0)
        add_p(1)

    def in_step(s):
        for p in range(2):
            for d in range(2):
                if ring_ok(p, d, s):
                    c_in(p, d, s).wait_recv()
                    if ring_ok(p, d, s + 1):
                        c_in(p, d, s + 1).start()

    scale = 0.03125

    def c_dn(m):
        rows = pl.ds(m * TILE, TILE)
        return pltpu.make_async_copy(dn.at[rows], dn_hbm.at[rows], osem.at[m])

    def mm_dn(m):
        cols = pl.ds(pl.multiple_of(m * TILE, TILE), TILE)
        lhs = acts[:, :, :, cols].reshape(1024, TILE)
        def half(n):
            oc = pl.ds(pl.multiple_of(n * 512, 512), 512)
            rhs = grads[:, :, :, :, oc].reshape(1024, 512)
            acc = lax.dot_general(lhs, rhs, TN, preferred_element_type=F32)
            dn[pl.ds(m * TILE, TILE), oc] = (acc * scale).astype(BF16)
        each(0, D // 512, half)
        c_dn(m).start()

    def hidden(h):
        each(1, 4, lambda dy: c_p2(h, dy).wait_recv())
        c_q2(h).wait_recv()

        def block(zz):
            acc = part[y, xh, zz, k, h].astype(F32) + prx[h, y, zz].astype(F32)
            for dy in range(1, 4):
                acc += p2r[h, dy, zz].astype(F32)
            hid[y, xh, zz, k, h] = (acc * slope[zz, k, h]).astype(BF16)
            acc = part[y, xh, zz, 1 - k, h].astype(F32) + q2r[h, zz].astype(F32)
            for dy in range(1, 4):
                acc += q1r[h, dy, xh, zz].astype(F32)
            hid[y, xh, zz, 1 - k, h] = (acc * slope[zz, 1 - k, h]).astype(BF16)

        each(0, 2, block)
        c_hidx(h).start()
        each(1, 4, lambda dy: c_hid(h, 0, dy).start())

    def relay(h):
        c_hidx(h).wait_recv()
        each(1, 4, lambda dy: c_hid(h, 1, dy).start())

        def one(dy):
            c_hid(h, 0, dy).wait_recv()
            c_hid(h, 2, dy).start()

        each(1, 4, one)

    each(1, ROWS, lambda o: c_act(o).wait_recv())
    c_inx().wait_recv()
    for d in range(2):
        c_in(1, d, 1).start()
    if H == 1:
        hidden(0)
        in_step(1)
        mm_dn(0)
        relay(0)
        in_step(2)
        mm_dn(1)
        mm_dn(2)
    else:
        hidden(0)
        add_q(1)
        mm_dn(0)
        in_step(1)
        hidden(1)
        relay(0)
        mm_dn(1)
        in_step(2)
        relay(1)

    def mm_ig(h, c):
        first = 2 * (1 - xl) if c == 0 else 2 * xl
        def tile(n):
            cols = pl.ds(pl.multiple_of(n * TILE, TILE), TILE)
            lhs = hid[pl.ds(first, 2), :, :, :, h].reshape(16 * R, F)
            acc = lax.dot_general(lhs, wup[cols, :], NT, preferred_element_type=F32).reshape(8, 2, R, TILE)
            igf[h, c, :, :, :, cols] = acc
            igs[h, c, :, :, :, cols] = acc.astype(BF16)
        each(0, D // TILE, tile)

    def share(h, o):
        j = z_at(o)
        igb[h, j] = (igf[h, 0, j, k] + igr[h, 0, j].astype(F32)).astype(BF16)
        c_igx(h, o).start()

    def pass_on(h, o):
        j = z_at(o)
        c_igx(h, o).wait_recv()
        acc = igf[h, 1, j, k] + igr[h, 1, j].astype(F32) + igx[h, j].astype(F32)
        if o == 0:
            igo[h] = acc
        else:
            igz[h, j] = acc.astype(BF16)
            c_ig(h, o).start()

    order = (4, 3, 5, 2, 6, 1, 7, 0)

    def ig(h):
        each(1, 4, lambda dy: c_hid(h, 1, dy).wait_recv())
        each(1, 4, lambda dy: c_hid(h, 2, dy).wait_recv())
        mm_ig(h, 0)
        c_igs(h, 0).start()
        mm_ig(h, 1)
        c_igs(h, 1).start()
        c_igs(h, 0).wait_recv()
        for o in order:
            share(h, o)

    wup_copy.wait()
    ig(0)
    in_step(3)
    if H == 2:
        ig(1)
        c_igs(0, 1).wait_recv()
        for i, o in enumerate(order):
            pass_on(0, o)
            if i == 3:
                in_step(4)
                c_inf().start()
        mm_dn(2)
    else:
        in_step(4)
        c_inf().start()
    c_igs(H - 1, 1).wait_recv()

    def c_up(m):
        rows = pl.ds(m * TILE, TILE)
        return pltpu.make_async_copy(up.at[rows], up_hbm.at[rows], osem.at[F // TILE + m])

    def mm_up(m):
        cols = pl.ds(pl.multiple_of(m * TILE, TILE), TILE)
        lhs = ins[:, :, :, cols].reshape(1024, TILE)
        rhs = hid[...].reshape(1024, F)
        acc = lax.dot_general(lhs, rhs, TN, preferred_element_type=F32)
        up[pl.ds(m * TILE, TILE), :] = (acc * scale).astype(BF16)
        c_up(m).start()

    for i, o in enumerate(order):
        pass_on(H - 1, o)
        if i == 0:
            c_inf().wait_recv()
        if i < D // TILE:
            mm_up(i)

    for h in range(H):
        each(1, 8, lambda o: c_ig(h, o).wait_recv())

        def total(n):
            cols = pl.ds(pl.multiple_of(n * 512, 512), 512)
            acc = igo[h, :, cols]
            for o in range(1, 8):
                acc += fin[o, h, :, cols].astype(F32)
            ig_out[pl.ds(h * R, R), cols] = acc.astype(BF16)

        each(0, D // 512, total)

    for p in range(2):
        for d in range(2):
            for t in range(1, 5):
                if ring_ok(p, d, t):
                    for h in range(H):
                        c_grad(h, p, d, t).wait_send()
                    c_in(p, d, t).wait_send()
    for h in range(H):
        c_gradx(h).wait_send()
        c_gradf(h).wait_send()
        c_px(h).wait_send()
        each(1, 4, lambda dy: c_p2(h, dy).wait_send())
        each(1, 4, lambda dy: c_q1(h, dy).wait_send())
        c_q2(h).wait_send()
        c_hidx(h).wait_send()
        for i in range(3):
            each(1, 4, lambda dy: c_hid(h, i, dy).wait_send())
        for c in range(2):
            c_igs(h, c).wait_send()
        each(0, 8, lambda o: c_igx(h, o).wait_send())
        each(1, 8, lambda o: c_ig(h, o).wait_send())
    c_inx().wait_send()
    c_inf().wait_send()
    each(1, ROWS, lambda o: c_act(o).wait_send())
    each(0, F // TILE, lambda m: c_dn(m).wait())
    each(0, D // TILE, lambda m: c_up(m).wait())


def copy_kernel(ig, up, dn, ig_out, up_out, dn_out, ig_v, up_v, dn_v, sem):
    steps = [(ig, ig_v, ig_out, pl.ds(0, ig.shape[0]))]
    for src, buf, dst in ((up, up_v, up_out), (dn, dn_v, dn_out)):
        n = src.shape[0] // 4
        steps += [(src, buf, dst, pl.ds(i * n, n)) for i in range(4)]
    loads = [pltpu.make_async_copy(s.at[r], v.at[r], sem.at[0, i]) for i, (s, v, d, r) in enumerate(steps)]
    stores = [pltpu.make_async_copy(v.at[r], d.at[r], sem.at[1, i]) for i, (s, v, d, r) in enumerate(steps)]
    for copy in loads:
        copy.start()
    for load, store in zip(loads, stores):
        load.wait()
        store.start()
    for copy in stores:
        copy.wait()


def per_device(H, inputs, out_grad, pre_act, w_up, w_down):
    R = 32 // H
    D = inputs.shape[1]
    F = pre_act.shape[1]
    vmem = pl.BlockSpec(memory_space=pltpu.VMEM)
    hbm = pl.BlockSpec(memory_space=pl.ANY)
    dma = pltpu.SemaphoreType.DMA
    shapes = (
        jax.ShapeDtypeStruct((32, D), BF16),
        jax.ShapeDtypeStruct((D, F), BF16),
        jax.ShapeDtypeStruct((F, D), BF16),
    )
    results = pl.pallas_call(
        functools.partial(kernel, H),
        out_shape=shapes,
        in_specs=[vmem, vmem, vmem, hbm, hbm],
        out_specs=(vmem, hbm, hbm),
        scratch_shapes=[
            pltpu.VMEM((D, F), BF16),
            pltpu.VMEM((F, D), BF16),
            pltpu.VMEM((2, 2, H, R, F), F32),
            pltpu.VMEM((COLS, 2, H, R, D), BF16),
            pltpu.VMEM((COLS, 2, 32, D), BF16),
            pltpu.VMEM((COLS, 2, 32, F), BF16),
            pltpu.VMEM((4, 2, 2, 2, H, R, F), BF16),
            pltpu.VMEM((H, 4, 2, R, F), BF16),
            pltpu.VMEM((H, 4, 2, R, F), BF16),
            pltpu.VMEM((H, 4, 2, R, F), BF16),
            pltpu.VMEM((H, 4, 2, 2, R, F), BF16),
            pltpu.VMEM((H, 2, R, F), BF16),
            pltpu.VMEM((H, 2, R, F), BF16),
            pltpu.VMEM((4, 2, 2, 2, H, R, F), BF16),
            pltpu.VMEM((H, 2, 8, 2, R, D), BF16),
            pltpu.VMEM((H, 2, 8, R, D), BF16),
            pltpu.VMEM((H, 2, 8, 2, R, D), F32),
            pltpu.VMEM((H, 8, R, D), BF16),
            pltpu.VMEM((H, 8, R, D), BF16),
            pltpu.VMEM((H, 8, R, D), BF16),
            pltpu.VMEM((H, R, D), F32),
            pltpu.VMEM((8, H, R, D), BF16),
            pltpu.VMEM((D, F), BF16),
            pltpu.VMEM((F, D), BF16),
            dma((2,)),
            dma((H,)), dma((H,)),
            dma((H, 16)), dma((H, 16)), dma((H,)), dma((H,)),
            dma, dma,
            dma((16,)), dma((16,)), dma, dma,
            dma((ROWS,)), dma((ROWS,)),
            dma((H,)), dma((H,)),
            dma((H, 4)), dma((H, 4)),
            dma((H, 4)), dma((H, 4)),
            dma((H,)), dma((H,)),
            dma((H, 3, 4)), dma((H, 3, 4)),
            dma((H,)), dma((H,)),
            dma((H, 2)), dma((H, 2)),
            dma((H, 8)), dma((H, 8)),
            dma((H, 8)), dma((H, 8)),
            dma((F // TILE + D // TILE,)),
        ],
        compiler_params=pltpu.CompilerParams(
            collective_id=0, has_side_effects=True, vmem_limit_bytes=56 * 2**20
        ),
        cost_estimate=pl.CostEstimate(flops=8 * 1024 * 1536 * 768, bytes_accessed=10 * 2**20, transcendentals=128 * 768),
    )(inputs, out_grad, pre_act, w_up, w_down)
    return pl.pallas_call(
        copy_kernel,
        out_shape=shapes,
        in_specs=[hbm] * 3,
        out_specs=(hbm,) * 3,
        scratch_shapes=[pltpu.VMEM(r.shape, BF16) for r in shapes] + [dma((2, 9))],
        compiler_params=pltpu.CompilerParams(vmem_limit_bytes=56 * 2**20),
    )(*results)


def solution(mesh):
    return jax.shard_map(
        functools.partial(per_device, 2),
        mesh=mesh,
        in_specs=(P("col", "row"), P("col", "row"), P("row", "col"), P("row", "col"), P("col", "row")),
        out_specs=(P("col", "row"), P("row", "col"), P("col", "row")),
        check_vma=False,
    )
```

```python
import functools

import jax
import jax.numpy as jnp
from jax import lax
from jax.experimental import pallas as pl
from jax.experimental.pallas import tpu as pltpu
from jax.sharding import PartitionSpec as P

MESH = pl.DeviceIdType.MESH
BF16 = jnp.bfloat16
F32 = jnp.float32
NT = (((1,), (1,)), ((), ()))
TN = (((0,), (0,)), ((), ()))
COLS = 16
ROWS = 8
TILE = 256


def kernel(
    H,
    in_ref, og_ref, pre_ref, wup_hbm, wdn_hbm,
    ig_out, up_hbm, dn_hbm,
    wup, wdn, slope, grads, ins, acts, part, prx, p2s, p2r, q1r, q2s, q2r, hid, igs, igr, igf, igb, igx, igz, igo, fin, up, dn,
    wsem, gys, gyr, gxs, gxr, gs, gr, gfs, gfr, xxs, xxr, xs, xr, xfs, xfr, as_, ar, pxs, pxr, p2ss, p2rs, q1ss, q1rs, q2ss, q2rs, hs, hr, hxs, hxr, ss, sr,
    bxs, bxr, is_, ir, axs, axr, osem,
):
    R = 32 // H
    D = in_ref.shape[1]
    F = pre_ref.shape[1]
    row = lax.axis_index("row")
    col = lax.axis_index("col")
    chip = lax.div(col, 2)
    k = lax.rem(col, 2)
    y, xh = lax.div(row, 2), lax.rem(row, 2)
    xl, z = lax.div(chip, 8), lax.rem(chip, 8)

    def z_at(dz):
        return lax.rem(z + dz, 8)

    def z_dev(dz):
        return (row, (xl * 8 + z_at(dz)) * 2 + k)

    other = (1 - xl) * 8
    partner = (row, (other + z) * 2 + k)

    def row_at(o):
        return lax.rem(y + o, 4) * 2 + lax.rem(xh + lax.div(o, 4), 2)

    def row_dev(o):
        return (row_at(o), col)

    def y_at(dy):
        return lax.rem(y + dy, 4)

    def y_dev(dy):
        return (y_at(dy) * 2 + xh, col)

    across = (y * 2 + 1 - xh, col)
    sib = (row, chip * 2 + 1 - k)

    def each(lo, hi, f):
        def body(o, carry):
            f(o)
            return carry
        lax.fori_loop(lo, hi, body, 0)

    def remote(src, dst, send, recv, dev):
        return pltpu.make_async_remote_copy(
            src_ref=src, dst_ref=dst, send_sem=send, recv_sem=recv, device_id=dev, device_id_type=MESH
        )

    wdn_copy = pltpu.make_async_copy(wdn_hbm, wdn, wsem.at[0])
    wup_copy = pltpu.make_async_copy(wup_hbm, wup, wsem.at[1])
    wdn_copy.start()
    wup_copy.start()

    barrier = pltpu.get_barrier_semaphore()
    each(1, 8, lambda o: pl.semaphore_signal(barrier, inc=1, device_id=z_dev(o), device_id_type=MESH))
    pl.semaphore_signal(barrier, inc=1, device_id=partner, device_id_type=MESH)
    each(1, ROWS, lambda o: pl.semaphore_signal(barrier, inc=1, device_id=row_dev(o), device_id_type=MESH))
    pl.semaphore_signal(barrier, inc=1, device_id=sib, device_id_type=MESH)
    pl.semaphore_wait(barrier, 7 + 1 + 1 + ROWS - 1)

    RING = {1: (0, 1), 2: (1, 1), 3: (2, 1), 4: (3, 1)}
    FAST = {1: (0, 1), 2: (0, 2), 3: (2, 1), 4: (2, 2)}

    def ring_block(way, p, d, s):
        back = way[s][0]
        return (xl * 8 if p == 0 else other) + z_at((8 - back) % 8 if d == 0 else back)

    def ring_dev(way, d, s):
        return z_dev(way[s][1] if d == 0 else 8 - way[s][1])

    def ring_ok(p, d, s):
        return s < 4 or (s == 4 and p == d)

    def grad_way(h):
        return RING

    def c_gradx(h):
        return remote(grads.at[chip, k, h], grads.at[chip, k, h], gxs.at[h], gxr.at[h], partner)

    def c_grad(h, p, d, s):
        block = grads.at[ring_block(grad_way(h), p, d, s), k, h]
        i = (p * 2 + d) * 4 + s - 1
        return remote(block, block, gs.at[h, i], gr.at[h, i], ring_dev(grad_way(h), d, s))

    def c_gx(d, s):
        block = grads.at[xl * 8 + z_at(8 - s if d == 0 else s), k, 1]
        return remote(block, block, gys.at[d * 4 + s - 1], gyr.at[d * 4 + s - 1], partner)

    def c_inx():
        return remote(ins.at[chip, k], ins.at[chip, k], xxs, xxr, partner)

    def c_in(p, d, s):
        block = ins.at[ring_block(RING, p, d, s), k]
        i = (p * 2 + d) * 4 + s - 1
        return remote(block, block, xs.at[i], xr.at[i], ring_dev(RING, d, s))

    def c_gradf(h):
        return remote(grads.at[:, k, h], grads.at[:, k, h], gfs.at[h], gfr.at[h], sib)

    def c_inf():
        return remote(ins.at[:, k], ins.at[:, k], xfs, xfr, sib)

    def c_actx():
        block = acts.at[pl.ds(2 * row, 2)]
        return remote(block, block, axs, axr, across)

    def c_act(p, dy):
        r = y * 2 + (xh if p == 0 else 1 - xh)
        block = acts.at[pl.ds(2 * r, 2)]
        return remote(block, block, as_.at[p, dy], ar.at[p, dy], y_dev(dy))

    def c_px(h):
        return remote(part.at[:, 1 - xh, :, k, h], prx.at[h], pxs.at[h], pxr.at[h], across)

    def c_p2(h, dy):
        return remote(p2s.at[h, dy], p2r.at[h, dy], p2ss.at[h, dy], p2rs.at[h, dy], y_dev(dy))

    def c_q1(h, dy):
        return remote(part.at[y_at(dy), :, :, 1 - k, h], q1r.at[h, dy], q1ss.at[h, dy], q1rs.at[h, dy], y_dev(dy))

    def c_q2(h):
        return remote(q2s.at[h], q2r.at[h], q2ss.at[h], q2rs.at[h], across)

    def c_hid(h, i, dy):
        if i == 0:
            block, dev = hid.at[y, xh, :, :, h], y_dev(dy)
        elif i == 1:
            block, dev = hid.at[y, 1 - xh, :, 0, h], y_dev(dy)
        else:
            block, dev = hid.at[y_at(4 - dy), xh, :, 1, h], across
        return remote(block, block, hs.at[h, i, dy], hr.at[h, i, dy], dev)

    def c_hidx(h):
        block = hid.at[y, xh, :, :, h]
        return remote(block, block, hxs.at[h], hxr.at[h], across)

    def c_igs(h, c):
        return remote(igs.at[h, c, :, 1 - k], igr.at[h, c], ss.at[h, c], sr.at[h, c], sib)

    def c_igx(h, o):
        return remote(igb.at[h, z_at(o)], igx.at[h, z_at(o)], bxs.at[h, o], bxr.at[h, o], partner)

    def c_ig(h, o):
        return remote(igz.at[h, z_at(o)], fin.at[o, h], is_.at[h, o], ir.at[h, o], z_dev(o))

    def grad_first(h, p):
        for s in (1, 2) if grad_way(h) is FAST else (1,):
            for d in range(2):
                c_grad(h, p, d, s).start()

    for h in range(H):
        grads[chip, k, h] = og_ref[h * R:(h + 1) * R]
        c_gradx(h).start()
        grad_first(h, 0)
    ins[chip, k] = in_ref[...]

    def gelu(b):
        hval = pre_ref[pl.ds(b * 32, 32), :].astype(F32)
        coeff = 0.7978845608028654
        inner = coeff * (hval + 0.044715 * hval * hval * hval)
        t = jnp.tanh(inner)
        act = (0.5 * hval * (1.0 + t)).astype(BF16)
        acts[2 * row + lax.div(b, 2), lax.rem(b, 2)] = act
        sl = 0.5 * (1.0 + t) + 0.5 * hval * (1.0 - t * t) * coeff * (1.0 + 3.0 * 0.044715 * hval * hval)
        for h in range(H):
            slope[lax.div(b, 2), lax.rem(b, 2), h] = sl[h * R:(h + 1) * R]

    each(0, 4, gelu)
    c_actx().start()
    each(1, 4, lambda dy: c_act(0, dy).start())

    def mm1(h, kk):
        def tile(n):
            cols = pl.ds(pl.multiple_of(n * TILE, TILE), TILE)
            lhs = grads[:, kk, h].reshape(16 * R, D)
            acc = lax.dot_general(lhs, wdn[cols, :], NT, preferred_element_type=F32)
            part[:, :, :, kk, h, :, cols] = acc.astype(BF16).reshape(4, 2, 2, R, TILE)
        each(0, F // TILE, tile)

    def grad_step(h, s):
        for p in range(2):
            for d in range(2):
                if ring_ok(p, d, s):
                    c_grad(h, p, d, s).wait_recv()
                    if ring_ok(p, d, s + 1):
                        c_grad(h, p, d, s + 1).start()

    def b_step(s):
        for d in range(2):
            if ring_ok(0, d, s):
                c_grad(1, 0, d, s).wait_recv()
                if ring_ok(0, d, s + 1):
                    c_grad(1, 0, d, s + 1).start()
                c_gx(d, s).start()

    def mm1_own(h):
        c_gradf(h).start()
        if h == 0:
            wdn_copy.wait()
        mm1(h, k)
        c_px(h).start()

    def mm1_sib(h):
        c_gradf(h).wait_recv()
        mm1(h, 1 - k)
        each(1, 4, lambda dy: c_q1(h, dy).start())

    def add_p(h):
        c_px(h).wait_recv()

        def one(dy):
            yy = y_at(dy)
            p2s[h, dy] = (part[yy, xh, :, k, h].astype(F32) + prx[h, yy].astype(F32)).astype(BF16)
            c_p2(h, dy).start()

        each(1, 4, one)

    def add_q(h):
        each(1, 4, lambda dy: c_q1(h, dy).wait_recv())
        acc = part[y, 1 - xh, :, 1 - k, h].astype(F32)
        for dy in range(1, 4):
            acc += q1r[h, dy, 1 - xh].astype(F32)
        q2s[h] = acc.astype(BF16)
        c_q2(h).start()

    def in_first():
        c_inx().start()
        for d in range(2):
            c_in(0, d, 1).start()

    c_gradx(0).wait_recv()
    grad_first(0, 1)
    c_actx().wait_recv()
    each(1, 4, lambda dy: c_act(1, dy).start())
    if H == 1:
        for s in range(1, 5):
            grad_step(0, s)
        in_first()
        mm1_own(0)
        mm1_sib(0)
        add_p(0)
        add_q(0)
    else:
        grad_step(0, 1)
        b_step(1)
        grad_step(0, 2)
        b_step(2)
        grad_step(0, 3)
        b_step(3)
        grad_step(0, 4)
        mm1_own(0)
        mm1_sib(0)
        b_step(4)
        c_gradx(1).wait_recv()
        for s in range(1, 5):
            for d in range(2):
                if ring_ok(0, d, s):
                    c_gx(d, s).wait_recv()
        mm1_own(1)
        in_first()
        add_p(0)
        mm1_sib(1)
        add_q(0)
        add_p(1)

    def in_step(s):
        for p in range(2):
            for d in range(2):
                if ring_ok(p, d, s):
                    c_in(p, d, s).wait_recv()
                    if ring_ok(p, d, s + 1):
                        c_in(p, d, s + 1).start()

    scale = 0.03125

    def c_dn(m):
        rows = pl.ds(m * TILE, TILE)
        return pltpu.make_async_copy(dn.at[rows], dn_hbm.at[rows], osem.at[m])

    def mm_dn(m):
        cols = pl.ds(pl.multiple_of(m * TILE, TILE), TILE)
        lhs = acts[:, :, :, cols].reshape(1024, TILE)
        def half(n):
            oc = pl.ds(pl.multiple_of(n * 512, 512), 512)
            rhs = grads[:, :, :, :, oc].reshape(1024, 512)
            acc = lax.dot_general(lhs, rhs, TN, preferred_element_type=F32)
            dn[pl.ds(m * TILE, TILE), oc] = (acc * scale).astype(BF16)
        each(0, D // 512, half)
        c_dn(m).start()

    def hidden(h):
        each(1, 4, lambda dy: c_p2(h, dy).wait_recv())
        c_q2(h).wait_recv()

        def block(zz):
            acc = part[y, xh, zz, k, h].astype(F32) + prx[h, y, zz].astype(F32)
            for dy in range(1, 4):
                acc += p2r[h, dy, zz].astype(F32)
            hid[y, xh, zz, k, h] = (acc * slope[zz, k, h]).astype(BF16)
            acc = part[y, xh, zz, 1 - k, h].astype(F32) + q2r[h, zz].astype(F32)
            for dy in range(1, 4):
                acc += q1r[h, dy, xh, zz].astype(F32)
            hid[y, xh, zz, 1 - k, h] = (acc * slope[zz, 1 - k, h]).astype(BF16)

        each(0, 2, block)
        c_hidx(h).start()
        each(1, 4, lambda dy: c_hid(h, 0, dy).start())

    def relay(h):
        c_hidx(h).wait_recv()
        each(1, 4, lambda dy: c_hid(h, 1, dy).start())

        def one(dy):
            c_hid(h, 0, dy).wait_recv()
            c_hid(h, 2, dy).start()

        each(1, 4, one)

    for p in range(2):
        each(1, 4, lambda dy: c_act(p, dy).wait_recv())
    c_inx().wait_recv()
    for d in range(2):
        c_in(1, d, 1).start()
    if H == 1:
        hidden(0)
        in_step(1)
        mm_dn(0)
        relay(0)
        in_step(2)
        mm_dn(1)
        mm_dn(2)
    else:
        hidden(0)
        add_q(1)
        mm_dn(0)
        in_step(1)
        hidden(1)
        relay(0)
        mm_dn(1)
        in_step(2)
        relay(1)

    def mm_ig(h, c):
        first = 2 * (1 - xl) if c == 0 else 2 * xl
        def tile(n):
            cols = pl.ds(pl.multiple_of(n * TILE, TILE), TILE)
            lhs = hid[pl.ds(first, 2), :, :, :, h].reshape(16 * R, F)
            acc = lax.dot_general(lhs, wup[cols, :], NT, preferred_element_type=F32).reshape(8, 2, R, TILE)
            igf[h, c, :, :, :, cols] = acc
            igs[h, c, :, :, :, cols] = acc.astype(BF16)
        each(0, D // TILE, tile)

    def share(h, o):
        j = z_at(o)
        igb[h, j] = (igf[h, 0, j, k] + igr[h, 0, j].astype(F32)).astype(BF16)
        c_igx(h, o).start()

    def pass_on(h, o):
        j = z_at(o)
        c_igx(h, o).wait_recv()
        acc = igf[h, 1, j, k] + igr[h, 1, j].astype(F32) + igx[h, j].astype(F32)
        if o == 0:
            igo[h] = acc
        else:
            igz[h, j] = acc.astype(BF16)
            c_ig(h, o).start()

    order = (4, 3, 5, 2, 6, 1, 7, 0)

    def ig(h):
        each(1, 4, lambda dy: c_hid(h, 1, dy).wait_recv())
        each(1, 4, lambda dy: c_hid(h, 2, dy).wait_recv())
        mm_ig(h, 0)
        c_igs(h, 0).start()
        mm_ig(h, 1)
        c_igs(h, 1).start()
        c_igs(h, 0).wait_recv()
        for o in order:
            share(h, o)

    wup_copy.wait()
    ig(0)
    in_step(3)
    if H == 2:
        ig(1)
        c_igs(0, 1).wait_recv()
        for i, o in enumerate(order):
            pass_on(0, o)
            if i == 3:
                in_step(4)
                c_inf().start()
        mm_dn(2)
    else:
        in_step(4)
        c_inf().start()
    c_igs(H - 1, 1).wait_recv()

    def c_up(m):
        rows = pl.ds(m * TILE, TILE)
        return pltpu.make_async_copy(up.at[rows], up_hbm.at[rows], osem.at[F // TILE + m])

    def mm_up(m):
        cols = pl.ds(pl.multiple_of(m * TILE, TILE), TILE)
        lhs = ins[:, :, :, cols].reshape(1024, TILE)
        rhs = hid[...].reshape(1024, F)
        acc = lax.dot_general(lhs, rhs, TN, preferred_element_type=F32)
        up[pl.ds(m * TILE, TILE), :] = (acc * scale).astype(BF16)
        c_up(m).start()

    for i, o in enumerate(order):
        pass_on(H - 1, o)
        if i == 0:
            c_inf().wait_recv()
        if i < D // TILE:
            mm_up(i)

    for h in range(H):
        each(1, 8, lambda o: c_ig(h, o).wait_recv())

        def total(n):
            cols = pl.ds(pl.multiple_of(n * 512, 512), 512)
            acc = igo[h, :, cols]
            for o in range(1, 8):
                acc += fin[o, h, :, cols].astype(F32)
            ig_out[pl.ds(h * R, R), cols] = acc.astype(BF16)

        each(0, D // 512, total)

    for p in range(2):
        for d in range(2):
            for t in range(1, 5):
                if ring_ok(p, d, t):
                    c_grad(0, p, d, t).wait_send()
                    if H == 2 and p == 0:
                        c_grad(1, 0, d, t).wait_send()
                        c_gx(d, t).wait_send()
                    c_in(p, d, t).wait_send()
    for h in range(H):
        c_gradx(h).wait_send()
        c_gradf(h).wait_send()
        c_px(h).wait_send()
        each(1, 4, lambda dy: c_p2(h, dy).wait_send())
        each(1, 4, lambda dy: c_q1(h, dy).wait_send())
        c_q2(h).wait_send()
        c_hidx(h).wait_send()
        for i in range(3):
            each(1, 4, lambda dy: c_hid(h, i, dy).wait_send())
        for c in range(2):
            c_igs(h, c).wait_send()
        each(0, 8, lambda o: c_igx(h, o).wait_send())
        each(1, 8, lambda o: c_ig(h, o).wait_send())
    c_inx().wait_send()
    c_inf().wait_send()
    c_actx().wait_send()
    for p in range(2):
        each(1, 4, lambda dy: c_act(p, dy).wait_send())
    each(0, F // TILE, lambda m: c_dn(m).wait())
    each(0, D // TILE, lambda m: c_up(m).wait())


def copy_kernel(ig, up, dn, ig_out, up_out, dn_out, ig_v, up_v, dn_v, sem):
    steps = [(ig, ig_v, ig_out, pl.ds(0, ig.shape[0]))]
    for src, buf, dst in ((up, up_v, up_out), (dn, dn_v, dn_out)):
        n = src.shape[0] // 4
        steps += [(src, buf, dst, pl.ds(i * n, n)) for i in range(4)]
    loads = [pltpu.make_async_copy(s.at[r], v.at[r], sem.at[0, i]) for i, (s, v, d, r) in enumerate(steps)]
    stores = [pltpu.make_async_copy(v.at[r], d.at[r], sem.at[1, i]) for i, (s, v, d, r) in enumerate(steps)]
    for copy in loads:
        copy.start()
    for load, store in zip(loads, stores):
        load.wait()
        store.start()
    for copy in stores:
        copy.wait()


def per_device(H, inputs, out_grad, pre_act, w_up, w_down):
    R = 32 // H
    D = inputs.shape[1]
    F = pre_act.shape[1]
    vmem = pl.BlockSpec(memory_space=pltpu.VMEM)
    hbm = pl.BlockSpec(memory_space=pl.ANY)
    dma = pltpu.SemaphoreType.DMA
    shapes = (
        jax.ShapeDtypeStruct((32, D), BF16),
        jax.ShapeDtypeStruct((D, F), BF16),
        jax.ShapeDtypeStruct((F, D), BF16),
    )
    results = pl.pallas_call(
        functools.partial(kernel, H),
        out_shape=shapes,
        in_specs=[vmem, vmem, vmem, hbm, hbm],
        out_specs=(vmem, hbm, hbm),
        scratch_shapes=[
            pltpu.VMEM((D, F), BF16),
            pltpu.VMEM((F, D), BF16),
            pltpu.VMEM((2, 2, H, R, F), F32),
            pltpu.VMEM((COLS, 2, H, R, D), BF16),
            pltpu.VMEM((COLS, 2, 32, D), BF16),
            pltpu.VMEM((COLS, 2, 32, F), BF16),
            pltpu.VMEM((4, 2, 2, 2, H, R, F), BF16),
            pltpu.VMEM((H, 4, 2, R, F), BF16),
            pltpu.VMEM((H, 4, 2, R, F), BF16),
            pltpu.VMEM((H, 4, 2, R, F), BF16),
            pltpu.VMEM((H, 4, 2, 2, R, F), BF16),
            pltpu.VMEM((H, 2, R, F), BF16),
            pltpu.VMEM((H, 2, R, F), BF16),
            pltpu.VMEM((4, 2, 2, 2, H, R, F), BF16),
            pltpu.VMEM((H, 2, 8, 2, R, D), BF16),
            pltpu.VMEM((H, 2, 8, R, D), BF16),
            pltpu.VMEM((H, 2, 8, 2, R, D), F32),
            pltpu.VMEM((H, 8, R, D), BF16),
            pltpu.VMEM((H, 8, R, D), BF16),
            pltpu.VMEM((H, 8, R, D), BF16),
            pltpu.VMEM((H, R, D), F32),
            pltpu.VMEM((8, H, R, D), BF16),
            pltpu.VMEM((D, F), BF16),
            pltpu.VMEM((F, D), BF16),
            dma((2,)),
            dma((8,)), dma((8,)),
            dma((H,)), dma((H,)),
            dma((H, 16)), dma((H, 16)), dma((H,)), dma((H,)),
            dma, dma,
            dma((16,)), dma((16,)), dma, dma,
            dma((2, 4)), dma((2, 4)),
            dma((H,)), dma((H,)),
            dma((H, 4)), dma((H, 4)),
            dma((H, 4)), dma((H, 4)),
            dma((H,)), dma((H,)),
            dma((H, 3, 4)), dma((H, 3, 4)),
            dma((H,)), dma((H,)),
            dma((H, 2)), dma((H, 2)),
            dma((H, 8)), dma((H, 8)),
            dma((H, 8)), dma((H, 8)),
            dma, dma,
            dma((F // TILE + D // TILE,)),
        ],
        compiler_params=pltpu.CompilerParams(
            collective_id=0, has_side_effects=True, vmem_limit_bytes=56 * 2**20
        ),
        cost_estimate=pl.CostEstimate(flops=8 * 1024 * 1536 * 768, bytes_accessed=10 * 2**20, transcendentals=128 * 768),
    )(inputs, out_grad, pre_act, w_up, w_down)
    return pl.pallas_call(
        copy_kernel,
        out_shape=shapes,
        in_specs=[hbm] * 3,
        out_specs=(hbm,) * 3,
        scratch_shapes=[pltpu.VMEM(r.shape, BF16) for r in shapes] + [dma((2, 9))],
        compiler_params=pltpu.CompilerParams(vmem_limit_bytes=56 * 2**20),
    )(*results)


def solution(mesh):
    return jax.shard_map(
        functools.partial(per_device, 2),
        mesh=mesh,
        in_specs=(P("col", "row"), P("col", "row"), P("row", "col"), P("row", "col"), P("col", "row")),
        out_specs=(P("col", "row"), P("row", "col"), P("col", "row")),
        check_vma=False,
    )
```
